256 devices in a mesh: tm: 8 (over z_lo, y), head: 32 (over x, z_hi, core).
Axes of the slice: x: 4, y: 4, z: 8 (z_hi: 4, z_lo: 2; z = z_hi * 2 + z_lo), core: 2. Of those that a mesh axis runs over, the one named last changes fastest.
Arguments:
- queries: bfloat16 [32768, 2048], P(('tm', 'head')), may hold values from -16 to 16
- key_rows: bfloat16 [32768, 2048], P(('tm', 'head')), may hold values from -16 to 16
- value_rows: bfloat16 [32768, 2048], P(('tm', 'head')), may hold values from -16 to 16
- grad_out: bfloat16 [32768, 2048], P(('tm', 'head')), may hold values from -16 to 16
- windows: int32 [128, 6], replicated, may hold values from -1 to 127, as said below
- tile_place: int32 [16, 8], replicated, may hold values from 0 to 7, each once within a row
Outputs:
- out: bfloat16 [32768, 2048], P(('tm', 'head'))
- dq: bfloat16 [32768, 2048], P(('tm', 'head'))
- dk: bfloat16 [32768, 2048], P(('tm', 'head'))
- dv: bfloat16 [32768, 2048], P(('tm', 'head'))
The draws below stay inside these ranges and needn't reach their ends.
Inputs may be any that keep to these rules, and one draw needn't show every extreme that they name: `windows`: row n lists the key tiles of natural tile n = 8 * t + 2 * y + x. Slots 2 * j and 2 * j + 1 hold a block of 2 tile rows by 1 tile column of time slice t - 1 + j that contains tile row y and column x, or -1 in both where that slice lies outside 0 to 15; tile n itself is always listed. `tile_place`: each row is a permutation of 0 to 7.
All inputs are finite; a program needn't handle non-finite values.
Results may differ from the reference program's by a relative error of at most 0.025.
Values may be sent and summed in bfloat16 or wider, within the bound.
A program may use at most 128 MiB of HBM per device.

```python
import jax
import jax.numpy as jnp
from jax import lax

HD = 128
HEADS = 16
TILE = 256
SH = 4
SW = 2
W = 6
SP = 8
NT = 16
NTILES = 128
TOKENS = 32768


def draw_queries(key, part):
    own_key = jax.random.fold_in(key, 1)
    return jnp.clip(jax.random.normal(own_key, (TOKENS, HEADS * HD), jnp.float32) * 1.4, -8.0, 8.0).astype(jnp.bfloat16)


def draw_key_rows(key, part):
    own_key = jax.random.fold_in(key, 2)
    return jnp.clip(jax.random.normal(own_key, (TOKENS, HEADS * HD), jnp.float32) * 1.4, -8.0, 8.0).astype(jnp.bfloat16)


def draw_windows(key, part):
    key = jax.random.fold_in(key, 7)
    tile_ids = jnp.arange(NTILES, dtype=jnp.int32)
    slice_of = tile_ids // (SH * SW)
    spatial_pos = tile_ids % (SH * SW)
    tile_row = spatial_pos // SW
    tile_col = spatial_pos % SW
    row_shift = jax.random.randint(key, (NTILES, 3), 0, 2)
    entries = []
    for time_step in range(3):
        target = slice_of + time_step - 1
        inside = (target >= 0) & (target < NT)
        first_row = jnp.clip(tile_row - row_shift[:, time_step], 0, SH - 2)
        for row_step in range(2):
            tile_named = target * (SH * SW) + (first_row + row_step) * SW + tile_col
            entries.append(jnp.where(inside, tile_named, -1))
    return jnp.stack(entries, axis=1).astype(jnp.int32)


def block_levels(key, dims, cuts, least, top_value):
    level, own = 1.0, jax.random.fold_in(key, 6)
    for position, parts in cuts:
        heights = jnp.exp(jax.random.uniform(jax.random.fold_in(own, position), (parts,), jnp.float32, least / len(cuts), top_value / len(cuts)))
        level = level * jnp.repeat(heights, dims[position] // parts).reshape([-1 if axis == position else 1 for axis in range(len(dims))])
    return level


def normal_values(stream_key, dims, deviation, most, cuts=(), kind=jnp.bfloat16):
    result = jax.random.normal(stream_key, dims, jnp.float32) * deviation
    if len(cuts) > 0:
        result = block_levels(stream_key, dims, cuts, -0.22, 0.18) * result
    return jnp.clip(result, min=-most, max=most).astype(kind)


def setup_inputs(seed: int = 0) -> dict:
    key_list = jax.random.split(jax.random.key(seed), 7)
    return {
        "queries": draw_queries(jax.random.fold_in(key_list[6], 71), 0),
        "key_rows": draw_key_rows(jax.random.fold_in(key_list[6], 71), 0),
        "value_rows": normal_values(key_list[2], (TOKENS, HEADS * HD), 4.0, 16.0, ((0, 256),)),
        "grad_out": normal_values(key_list[3], (TOKENS, HEADS * HD), 4.0, 16.0, ((0, 256),)),
        "windows": draw_windows(jax.random.fold_in(key_list[6], 71), 0),
        "tile_place": jax.vmap(lambda own: jax.random.permutation(own, SP))(jax.random.split(key_list[5], NT)).reshape((NT, SP)).astype(jnp.int32),
    }


def natural_tiles(tile_place):
    slice_total, spatial = tile_place.shape
    starts = jnp.arange(slice_total, dtype=jnp.int32)[:, None] * spatial
    return (starts + tile_place).reshape(slice_total * spatial).astype(jnp.int32)


def head_attention(query_tiles, key_tiles, value_tiles, grad_tiles, windows):
    usable = windows >= 0
    key_index = jnp.where(usable, windows, 0).astype(jnp.int32)
    logit_scale = HD ** -0.5
    block_tiles = 8
    tile_total = query_tiles.shape[0]
    steps_total = tile_total // block_tiles

    def regroup(tensor):
        return tensor.reshape((steps_total, block_tiles) + tensor.shape[1:])

    zero_grads = jnp.zeros((tile_total, TILE, HD), jnp.float32)

    def one_block(totals, pieces):
        total_keys, total_values = totals
        query_block_rows, gradient_block_rows, index_block, usable_block = pieces
        query_broad = query_block_rows.astype(jnp.float32)
        gradient_broad = gradient_block_rows.astype(jnp.float32)
        key_block_rows = key_tiles[index_block].reshape(block_tiles, W * TILE, HD).astype(jnp.float32)
        value_block_rows = value_tiles[index_block].reshape(block_tiles, W * TILE, HD).astype(jnp.float32)
        key_mask = jnp.repeat(usable_block, TILE, axis=1)[:, None, :]
        logit_matrix = jnp.einsum("ast,ait->asi", query_broad, key_block_rows) * logit_scale
        logit_matrix = jnp.where(key_mask, logit_matrix, -jnp.inf)
        row_peak = jnp.max(logit_matrix, axis=2, keepdims=True)
        raised = jnp.exp(logit_matrix - row_peak)
        soft_weights = raised / jnp.sum(raised, axis=2, keepdims=True)
        weight_narrow = soft_weights.astype(jnp.bfloat16)
        weight_broad = weight_narrow.astype(jnp.float32)
        output_block = jnp.einsum("aiw,awu->aiu", weight_broad, value_block_rows).astype(jnp.bfloat16)
        row_term = jnp.sum(gradient_broad * output_block.astype(jnp.float32), axis=2, keepdims=True)
        probability_gradient = jnp.einsum("ast,ait->asi", gradient_broad, value_block_rows)
        score_gradient_narrow = (soft_weights * (probability_gradient - row_term)).astype(jnp.bfloat16)
        score_gradient_broad = score_gradient_narrow.astype(jnp.float32)
        query_gradient_block = (jnp.einsum("aiw,awu->aiu", score_gradient_broad, key_block_rows) * logit_scale).astype(jnp.bfloat16)
        key_gradient_terms = jnp.einsum("iuy,iuh->iyh", score_gradient_broad, query_broad) * logit_scale
        value_gradient_terms = jnp.einsum("iuy,iuh->iyh", weight_broad, gradient_broad)
        flat_index = index_block.reshape(block_tiles * W)
        total_keys = total_keys.at[flat_index].add(key_gradient_terms.reshape(block_tiles * W, TILE, HD))
        total_values = total_values.at[flat_index].add(value_gradient_terms.reshape(block_tiles * W, TILE, HD))
        return (total_keys, total_values), (output_block, query_gradient_block)

    (total_keys, total_values), (out_blocks, dq_blocks) = lax.scan(
        one_block, (zero_grads, zero_grads),
        (regroup(query_tiles), regroup(grad_tiles), regroup(key_index), regroup(usable)))
    out_tiles = out_blocks.reshape(tile_total, TILE, HD)
    dq_tiles = dq_blocks.reshape(tile_total, TILE, HD)
    return out_tiles, dq_tiles, total_keys.astype(jnp.bfloat16), total_values.astype(jnp.bfloat16)


def reference(queries, key_rows, value_rows, grad_out, windows, tile_place):
    natural = natural_tiles(tile_place)
    inverse = jnp.argsort(natural).astype(jnp.int32)

    def per_head(head_number):
        def columns(tensor):
            columns_part = lax.dynamic_slice_in_dim(tensor, head_number * HD, HD, 1)
            return columns_part.reshape(NTILES, TILE, HD)[inverse]

        results = head_attention(columns(queries), columns(key_rows), columns(value_rows), columns(grad_out), windows)
        return tuple(result_item[natural].reshape(TOKENS, HD) for result_item in results)

    stacked = lax.map(per_head, jnp.arange(HEADS, dtype=jnp.int32))

    def assemble(tensor):
        return jnp.transpose(tensor, (1, 0, 2)).reshape(TOKENS, HEADS * HD)

    return assemble(stacked[0]), assemble(stacked[1]), assemble(stacked[2]), assemble(stacked[3])
```

```python
import functools

import jax
import jax.numpy as jnp
import numpy as np
from jax import lax
from jax.sharding import PartitionSpec as P
import jax.experimental.pallas as pl
import jax.experimental.pallas.tpu as pltpu

HD = 128
HEADS = 16
TILE = 256
SP = 8
W = 6
HALF = 128
NONE = SP * W
MESH = pl.DeviceIdType.MESH
BF = jnp.bfloat16
F32 = jnp.float32
SCALE = HD**-0.5
SCALE2 = float(SCALE * np.log2(np.e))
NN = (((1,), (0,)), ((), ()))
TN = (((0,), (0,)), ((), ()))


def dot(a, b, dims):
    return lax.dot_general(a, b, dims, preferred_element_type=F32)


def place():
    group = lax.axis_index("tm")
    index = lax.axis_index("head")
    return group, index, index // HEADS, lax.rem(index, HEADS), index // 2, lax.rem(index, 2)


def around():
    group, index, _, _, _, core = place()
    other = index + 1 - 2 * core
    before = (group - 1 + core, other)
    after = (group + core, other)
    has_before = (core == 1) | (group > 0)
    has_after = (core == 0) | (group < lax.axis_size("tm") - 1)
    return before, after, has_before, has_after


def greet():
    group, index, half, _, _, core = place()
    barrier = pltpu.get_barrier_semaphore()

    def signal(i, carry):
        for other in (2 * i + half, HEADS * core + i):

            @pl.when(other != index)
            def _():
                pl.semaphore_signal(barrier, 1, device_id=(group, other), device_id_type=MESH)

        return carry

    lax.fori_loop(0, HEADS, signal, 0)
    before, after, has_before, has_after = around()

    @pl.when(has_before)
    def _():
        pl.semaphore_signal(barrier, 1, device_id=before, device_id_type=MESH)

    @pl.when(has_after)
    def _():
        pl.semaphore_signal(barrier, 1, device_id=after, device_id_type=MESH)

    own = jnp.where(half == core, 2, 0)
    pl.semaphore_wait(barrier, 2 * HEADS - own + has_before.astype(jnp.int32) + has_after.astype(jnp.int32))


def landed(ref, sem):
    pltpu.make_async_copy(ref, ref, sem).wait()


def send(src, dst, send_sem, recv_sem, target):
    pltpu.make_async_remote_copy(
        src_ref=src, dst_ref=dst, send_sem=send_sem, recv_sem=recv_sem, device_id=target, device_id_type=MESH
    ).start()


def half_rows(ref, i, first=0):
    return ref.at[first + i // 2, pl.ds(pl.multiple_of(lax.rem(i, 2) * HALF, HALF), HALF)]


def head_columns(ref, h):
    return ref.at[:, pl.ds(pl.multiple_of(h * HD, HD), HD)]


def loop(n, step):
    def body(i, carry):
        step(i)
        return carry

    lax.fori_loop(0, n, body, 0)


def gather_kernel(q_in, k_in, v_in, g_in, q, kx, vx, g, sent, got, halo_sent, halo_got):
    group, index, half, mine, head, core = place()
    greet()
    arrays = ((k_in, kx, SP), (v_in, vx, SP), (q_in, q, 0), (g_in, g, 0))
    for a, (src, dst, first) in enumerate(arrays):

        def push(n):
            h = lax.rem(head + n, HEADS)
            target = 2 * h + half

            @pl.when(target != index)
            def _():
                send(
                    head_columns(src, h),
                    half_rows(dst, mine, first),
                    sent.at[a, n],
                    got.at[a, mine],
                    (group, target),
                )

            @pl.when(target == index)
            def _():
                pltpu.make_async_copy(head_columns(src, h), half_rows(dst, mine, first), got.at[a, mine]).start()

        loop(HEADS, push)

    before, after, has_before, has_after = around()
    for a, (src, dst, first) in enumerate(arrays):
        loop(HEADS, lambda i: landed(half_rows(dst, i, first), got.at[a, i]))
        if a < 2:
            own = dst.at[pl.ds(SP, SP)]

            @pl.when(has_before)
            def _():
                send(own, dst.at[pl.ds(2 * SP, SP)], halo_sent.at[a, 0], halo_got.at[a, 1], before)

            @pl.when(has_after)
            def _():
                send(own, dst.at[pl.ds(0, SP)], halo_sent.at[a, 1], halo_got.at[a, 0], after)

    for a, dst in enumerate((kx, vx)):
        own = dst.at[pl.ds(SP, SP)]

        @pl.when(has_before)
        def _():
            landed(dst.at[pl.ds(0, SP)], halo_got.at[a, 0])
            landed(own, halo_sent.at[a, 0])

        @pl.when(has_after)
        def _():
            landed(dst.at[pl.ds(2 * SP, SP)], halo_got.at[a, 1])
            landed(own, halo_sent.at[a, 1])

    for a, (src, dst, first) in enumerate(arrays):

        def drain(n):
            h = lax.rem(head + n, HEADS)

            @pl.when(2 * h + half != index)
            def _():
                landed(half_rows(dst, mine, first), sent.at[a, n])

        loop(HEADS, drain)


def tables(windows, tile_place, inverse, key_at, usable, query_of, pair_of):
    group, _, _, _, _, core = place()
    slice_id = 2 * group + core
    last = 2 * lax.axis_size("tm") - 1

    def invert(n):
        near = jnp.clip(slice_id - 1 + n // SP, 0, last)
        tile = lax.rem(n, SP)
        found = jnp.int32(0)
        for i in range(SP):
            found = found + jnp.where(tile_place[near, i] == tile, i, 0)
        inverse[n] = found

    loop(3 * SP, invert)

    def query(n):
        i = n // W
        w = lax.rem(n, W)
        tile = SP * slice_id + tile_place[slice_id, i]
        listed = windows[tile, w]
        good = listed >= 0
        named = jnp.where(good, listed, windows[tile, 2])
        key_at[n] = inverse[named - SP * (slice_id - 1)] + SP * jnp.where(good, w // 2, 1)
        usable[n] = good.astype(jnp.int32)

    loop(SP * W, query)

    def key(n):
        m = n // 3
        j = m // SP
        near = jnp.clip(slice_id - 1 + j, 0, last)
        tile = tile_place[near, lax.rem(m, SP)]
        row = tile // 2 + lax.rem(n, 3) - 1
        inside = (row >= 0) & (row < SP // 2)
        asker = jnp.where(inside, 2 * row + lax.rem(tile, 2), 0)
        i = inverse[SP + asker]
        name = SP * near + tile
        first = windows[SP * slice_id + asker, 2 * j] == name
        second = windows[SP * slice_id + asker, 2 * j + 1] == name
        query_of[n] = i
        pair_of[n] = jnp.where(
            inside & (first | second), i * W + 2 * j + jnp.where(second, 1, 0), NONE
        )

    loop(9 * SP, key)


def query_tile(i, key_at, usable, q, g, kx, vx, o, dq, probs, dscores, q_scaled, g_scaled):
    q_rows = q[i]
    g_rows = g[i]
    q_turned = q_rows.T
    g_turned = g_rows.T
    at = [key_at[i * W + w] for w in range(W)]
    scores = [dot(kx[at[w]], q_turned, NN) for w in range(W)]
    peak = scores[0]
    for w in range(1, W):
        peak = jnp.maximum(peak, scores[w])
    peak = jnp.max(peak, axis=0, keepdims=True) * SCALE2
    total = jnp.zeros((1, TILE), F32)
    out = jnp.zeros((HD, TILE), F32)
    raised = []
    for w in range(W):
        level = peak + jnp.where(usable[i * W + w] > 0, 0.0, 1e30)
        e = jnp.exp2(scores[w] * SCALE2 - level)
        total = total + jnp.sum(e, axis=0, keepdims=True)
        low = e.astype(BF)
        probs[i * W + w] = low
        raised.append(e)
        out = out + dot(vx[at[w]], low, TN)
    share = 1.0 / total
    out_low = (out * share).astype(BF)
    o[i] = out_low.T
    row_term = jnp.sum(g_turned.astype(F32) * out_low.astype(F32), axis=0, keepdims=True)
    grad = jnp.zeros((HD, TILE), F32)
    for w in range(W):
        dprobs = dot(vx[at[w]], g_turned, NN)
        low = (raised[w] * (dprobs - row_term)).astype(BF)
        dscores[i * W + w] = low
        grad = grad + dot(kx[at[w]], low, TN)
    dq[i] = (grad * (share * SCALE)).astype(BF).T
    share_rows = jnp.transpose(jnp.broadcast_to(share, (HD, TILE)))
    q_scaled[i] = (q_rows.astype(F32) * (share_rows * SCALE)).astype(BF)
    g_scaled[i] = (g_rows.astype(F32) * share_rows).astype(BF)


def key_tile(m, query_of, pair_of, q_scaled, g_scaled, probs, dscores):
    grad_k = jnp.zeros((TILE, HD), F32)
    grad_v = jnp.zeros((TILE, HD), F32)
    for n in range(3):
        i = query_of[3 * m + n]
        pair = pair_of[3 * m + n]
        grad_v = grad_v + dot(probs[pair], g_scaled[i], NN)
        grad_k = grad_k + dot(dscores[pair], q_scaled[i], NN)
    return grad_k, grad_v


def compute_kernel(
    windows, tile_place, q, kx, vx, g, o, dq, dk, dv, dk_far, dv_far,
    inverse, key_at, usable, query_of, pair_of, probs, dscores, q_scaled, g_scaled,
):
    tables(windows, tile_place, inverse, key_at, usable, query_of, pair_of)
    probs[NONE] = jnp.zeros((TILE, TILE), BF)
    dscores[NONE] = jnp.zeros((TILE, TILE), BF)
    loop(SP, lambda i: query_tile(i, key_at, usable, q, g, kx, vx, o, dq, probs, dscores, q_scaled, g_scaled))

    def own(m):
        dk[m], dv[m] = key_tile(SP + m, query_of, pair_of, q_scaled, g_scaled, probs, dscores)

    def far(n):
        m = jnp.where(n < SP, n, n + SP)
        grad_k, grad_v = key_tile(m, query_of, pair_of, q_scaled, g_scaled, probs, dscores)
        dk_far[n] = grad_k.astype(BF)
        dv_far[n] = grad_v.astype(BF)

    loop(2 * SP, far)
    loop(SP, own)


def return_kernel(
    o, dq, dk, dv, dk_far, dv_far, o_out, dq_out, dk_out, dv_out,
    dk_near, dv_near, dk_low, dv_low, sent, got, halo_sent, halo_got,
):
    group, index, half, mine, head, core = place()
    greet()
    before, after, has_before, has_after = around()
    for a, (far, near) in enumerate(((dk_far, dk_near), (dv_far, dv_near))):

        @pl.when(has_before)
        def _():
            send(far.at[pl.ds(0, SP)], near.at[pl.ds(SP, SP)], halo_sent.at[a, 0], halo_got.at[a, 1], before)

        @pl.when(has_after)
        def _():
            send(far.at[pl.ds(SP, SP)], near.at[pl.ds(0, SP)], halo_sent.at[a, 1], halo_got.at[a, 0], after)

    def push_all(a, src, dst):
        def push(n):
            i = lax.rem(mine + n, HEADS)
            target = HEADS * core + i

            @pl.when(target != index)
            def _():
                send(half_rows(src, i), head_columns(dst, head), sent.at[a, n], got.at[a, head], (group, target))

            @pl.when(target == index)
            def _():
                pltpu.make_async_copy(half_rows(src, i), head_columns(dst, head), got.at[a, head]).start()

        loop(HEADS, push)

    push_all(0, o, o_out)
    push_all(1, dq, dq_out)

    sums = ((dk, dk_far, dk_near, dk_low, dk_out), (dv, dv_far, dv_near, dv_low, dv_out))
    for a, (full, far, near, low, out) in enumerate(sums):

        @pl.when(has_before)
        def _():
            landed(near.at[pl.ds(0, SP)], halo_got.at[a, 0])
            landed(far.at[pl.ds(0, SP)], halo_sent.at[a, 0])

        @pl.when(jnp.logical_not(has_before))
        def _():
            near[pl.ds(0, SP)] = jnp.zeros((SP, TILE, HD), BF)

        @pl.when(has_after)
        def _():
            landed(near.at[pl.ds(SP, SP)], halo_got.at[a, 1])
            landed(far.at[pl.ds(SP, SP)], halo_sent.at[a, 1])

        @pl.when(jnp.logical_not(has_after))
        def _():
            near[pl.ds(SP, SP)] = jnp.zeros((SP, TILE, HD), BF)

        def add(m):
            low[m] = (full[m] + near[m].astype(F32) + near[SP + m].astype(F32)).astype(BF)

        loop(SP, add)
        push_all(2 + a, low, out)

    for a, (src, dst) in enumerate(((o, o_out), (dq, dq_out), (dk_low, dk_out), (dv_low, dv_out))):

        def drain(n):
            landed(head_columns(dst, n), got.at[a, n])
            i = lax.rem(mine + n, HEADS)

            @pl.when(HEADS * core + i != index)
            def _():
                landed(half_rows(src, i), sent.at[a, n])

        loop(HEADS, drain)


def body(queries, key_rows, value_rows, grad_out, windows, tile_place):
    anywhere = pl.BlockSpec(memory_space=pl.ANY)
    vmem = pl.BlockSpec(memory_space=pltpu.VMEM)
    smem = pl.BlockSpec(memory_space=pltpu.SMEM)
    tiles = lambda n, kind=BF: jax.ShapeDtypeStruct((n, TILE, HD), kind)
    rows = jax.ShapeDtypeStruct(queries.shape, BF)
    dma = pltpu.SemaphoreType.DMA
    limit = 56 * 1024 * 1024

    q, kx, vx, g = pl.pallas_call(
        gather_kernel,
        out_shape=[tiles(SP), tiles(3 * SP), tiles(3 * SP), tiles(SP)],
        in_specs=[anywhere] * 4,
        out_specs=[vmem] * 4,
        scratch_shapes=[dma((4, HEADS)), dma((4, HEADS)), dma((2, 2)), dma((2, 2))],
        compiler_params=pltpu.CompilerParams(collective_id=0, has_side_effects=True, vmem_limit_bytes=limit),
        name="gather",
    )(queries, key_rows, value_rows, grad_out)

    o, dq, dk, dv, dk_far, dv_far = pl.pallas_call(
        compute_kernel,
        out_shape=[tiles(SP), tiles(SP), tiles(SP, F32), tiles(SP, F32), tiles(2 * SP), tiles(2 * SP)],
        in_specs=[smem] * 2 + [vmem] * 4,
        out_specs=[vmem] * 6,
        scratch_shapes=[
            pltpu.SMEM((3 * SP,), jnp.int32),
            pltpu.SMEM((SP * W,), jnp.int32),
            pltpu.SMEM((SP * W,), jnp.int32),
            pltpu.SMEM((9 * SP,), jnp.int32),
            pltpu.SMEM((9 * SP,), jnp.int32),
            pltpu.VMEM((NONE + 1, TILE, TILE), BF),
            pltpu.VMEM((NONE + 1, TILE, TILE), BF),
            pltpu.VMEM((SP, TILE, HD), BF),
            pltpu.VMEM((SP, TILE, HD), BF),
        ],
        compiler_params=pltpu.CompilerParams(vmem_limit_bytes=limit),
        name="compute",
    )(windows, tile_place, q, kx, vx, g)

    return pl.pallas_call(
        return_kernel,
        out_shape=[rows] * 4,
        in_specs=[vmem] * 6,
        out_specs=[anywhere] * 4,
        scratch_shapes=[
            pltpu.VMEM((2 * SP, TILE, HD), BF),
            pltpu.VMEM((2 * SP, TILE, HD), BF),
            pltpu.VMEM((SP, TILE, HD), BF),
            pltpu.VMEM((SP, TILE, HD), BF),
            dma((4, HEADS)),
            dma((4, HEADS)),
            dma((2, 2)),
            dma((2, 2)),
        ],
        compiler_params=pltpu.CompilerParams(collective_id=1, has_side_effects=True, vmem_limit_bytes=limit),
        name="send_back",
    )(o, dq, dk, dv, dk_far, dv_far)


def solution(mesh):
    spread = P(("tm", "head"), None)
    return jax.shard_map(
        body,
        mesh=mesh,
        in_specs=(spread,) * 4 + (P(), P()),
        out_specs=(spread,) * 4,
        check_vma=False,
    )
```

```python
import functools

import jax
import jax.numpy as jnp
import numpy as np
from jax import lax
from jax.sharding import PartitionSpec as P
import jax.experimental.pallas as pl
import jax.experimental.pallas.tpu as pltpu

HD = 128
HEADS = 16
TILE = 256
SP = 8
W = 6
HALF = 128
NONE = SP * W
MESH = pl.DeviceIdType.MESH
BF = jnp.bfloat16
F32 = jnp.float32
SCALE = HD**-0.5
SCALE2 = float(SCALE * np.log2(np.e))
NN = (((1,), (0,)), ((), ()))
TN = (((0,), (0,)), ((), ()))


def dot(a, b, dims):
    return lax.dot_general(a, b, dims, preferred_element_type=F32)


class Place:
    def __init__(self):
        self.tm = lax.axis_index("tm")
        self.index = lax.axis_index("head")
        self.low, self.y = self.tm // 4, lax.rem(self.tm, 4)
        x = self.index // 8
        z = 2 * lax.rem(self.index // 2, 4) + self.low
        self.half, self.mine = self.index // HEADS, lax.rem(self.index, HEADS)
        self.core = lax.rem(self.index, 2)
        self.head = 8 * (x // 2) + z
        self.group = 4 * lax.rem(x + z, 2) + self.y
        self.slice = 2 * self.group + self.core
        self.last = 2 * lax.axis_size("tm") - 1
        self.stays = (self.group == self.tm) & (self.core == self.half)

    def worker(self, group, head, core):
        z = lax.rem(head, 8)
        x = 2 * (head // 8) + lax.rem(group // 4 + z, 2)
        return 4 * lax.rem(z, 2) + lax.rem(group, 4), 8 * x + 2 * (z // 2) + core

    def worker_of_mine(self, head):
        return self.worker(self.tm, head, self.half)

    def holder(self, i):
        return self.group, HEADS * self.core + i

    def is_me(self, device):
        return (device[0] == self.tm) & (device[1] == self.index)

    def nth_head(self, n):
        step = n // 2
        far = (step + 1) // 2
        turn = jnp.where(lax.rem(step, 2) == 1, far, 8 - far)
        return 8 * lax.rem(self.head // 8 + n, 2) + lax.rem(self.head + turn, 8)

    def before(self):
        return self.worker(self.group - 1 + self.core, self.head, 1 - self.core)

    def after(self):
        return self.worker(self.group + self.core, self.head, 1 - self.core)


def greet(me):
    barrier = pltpu.get_barrier_semaphore()

    def signal(i):
        for other in (me.worker_of_mine(i), me.holder(i)):

            @pl.when(jnp.logical_not(me.is_me(other)))
            def _():
                pl.semaphore_signal(barrier, 1, device_id=other, device_id_type=MESH)

    loop(HEADS, signal)
    has_before, has_after = me.slice > 0, me.slice < me.last

    @pl.when(has_before)
    def _():
        pl.semaphore_signal(barrier, 1, device_id=me.before(), device_id_type=MESH)

    @pl.when(has_after)
    def _():
        pl.semaphore_signal(barrier, 1, device_id=me.after(), device_id_type=MESH)

    own = jnp.where(me.stays, 2, 0)
    pl.semaphore_wait(barrier, 2 * HEADS - own + has_before.astype(jnp.int32) + has_after.astype(jnp.int32))


def landed(ref, sem):
    pltpu.make_async_copy(ref, ref, sem).wait()


def send(src, dst, send_sem, recv_sem, target):
    pltpu.make_async_remote_copy(
        src_ref=src, dst_ref=dst, send_sem=send_sem, recv_sem=recv_sem, device_id=target, device_id_type=MESH
    ).start()


def half_rows(ref, i, first=0):
    return ref.at[first + i // 2, pl.ds(pl.multiple_of(lax.rem(i, 2) * HALF, HALF), HALF)]


def head_columns(ref, h):
    return ref.at[:, pl.ds(pl.multiple_of(h * HD, HD), HD)]


def loop(n, step):
    def body(i, carry):
        step(i)
        return carry

    lax.fori_loop(0, n, body, 0)


def tables(me, windows, tile_place, inverse, key_at, usable, query_of, pair_of):
    slice_id, last = me.slice, me.last

    def invert(n):
        near = jnp.clip(slice_id - 1 + n // SP, 0, last)
        tile = lax.rem(n, SP)
        found = jnp.int32(0)
        for i in range(SP):
            found = jnp.where(tile_place[near, i] == tile, i, found)
        inverse[n] = found

    loop(3 * SP, invert)

    def query(n):
        i = n // W
        w = lax.rem(n, W)
        tile = SP * slice_id + jnp.clip(tile_place[slice_id, i], 0, SP - 1)
        listed = windows[tile, w]
        good = listed >= 0
        named = jnp.where(good, listed, windows[tile, 2])
        near = jnp.clip(named - SP * (slice_id - 1), 0, 3 * SP - 1)
        key_at[n] = inverse[near] + SP * jnp.where(good, w // 2, 1)
        usable[n] = good.astype(jnp.int32)

    loop(SP * W, query)

    def key(n):
        m = n // 3
        j = m // SP
        near = jnp.clip(slice_id - 1 + j, 0, last)
        tile = jnp.clip(tile_place[near, lax.rem(m, SP)], 0, SP - 1)
        row = tile // 2 + lax.rem(n, 3) - 1
        inside = (row >= 0) & (row < SP // 2)
        asker = jnp.where(inside, 2 * row + lax.rem(tile, 2), 0)
        i = inverse[SP + asker]
        name = SP * near + tile
        first = windows[SP * slice_id + asker, 2 * j] == name
        second = windows[SP * slice_id + asker, 2 * j + 1] == name
        query_of[n] = i
        pair_of[n] = jnp.where(
            inside & (first | second), i * W + 2 * j + jnp.where(second, 1, 0), NONE
        )

    loop(9 * SP, key)


def query_tile(i, key_at, usable, q, g, kx, vx, o, dq, probs, dscores, q_scaled, g_scaled):
    q_rows = q[i]
    g_rows = g[i]
    q_turned = q_rows.T
    g_turned = g_rows.T
    at = [key_at[i * W + w] for w in range(W)]
    scores = [dot(kx[at[w]], q_turned, NN) for w in range(W)]
    peak = scores[0]
    for w in range(1, W):
        peak = jnp.maximum(peak, scores[w])
    peak = jnp.max(peak, axis=0, keepdims=True) * SCALE2
    total = jnp.zeros((1, TILE), F32)
    out = jnp.zeros((HD, TILE), F32)
    raised = []
    for w in range(W):
        level = peak + jnp.where(usable[i * W + w] > 0, 0.0, 1e30)
        e = jnp.exp2(scores[w] * SCALE2 - level)
        total = total + jnp.sum(e, axis=0, keepdims=True)
        low = e.astype(BF)
        probs[i * W + w] = low
        raised.append(e)
        out = out + dot(vx[at[w]], low, TN)
    share = 1.0 / total
    out_low = (out * share).astype(BF)
    o[i] = out_low.T
    row_term = jnp.sum(g_turned.astype(F32) * out_low.astype(F32), axis=0, keepdims=True)
    grad = jnp.zeros((HD, TILE), F32)
    for w in range(W):
        dprobs = dot(vx[at[w]], g_turned, NN)
        low = (raised[w] * (dprobs - row_term)).astype(BF)
        dscores[i * W + w] = low
        grad = grad + dot(kx[at[w]], low, TN)
    dq[i] = (grad * (share * SCALE)).astype(BF).T
    share_rows = jnp.transpose(jnp.broadcast_to(share, (HD, TILE)))
    q_scaled[i] = (q_rows.astype(F32) * (share_rows * SCALE)).astype(BF)
    g_scaled[i] = (g_rows.astype(F32) * share_rows).astype(BF)


def key_tile(m, query_of, pair_of, q_scaled, g_scaled, probs, dscores):
    grad_k = jnp.zeros((TILE, HD), F32)
    grad_v = jnp.zeros((TILE, HD), F32)
    for n in range(3):
        i = query_of[3 * m + n]
        pair = pair_of[3 * m + n]
        grad_v = grad_v + dot(probs[pair], g_scaled[i], NN)
        grad_k = grad_k + dot(dscores[pair], q_scaled[i], NN)
    return grad_k, grad_v


def attention_kernel(
    windows, tile_place, q_in, k_in, v_in, g_in, o_out, dq_out, dk_out, dv_out,
    q, kx, vx, g, o, dq, probs, dscores, q_scaled, g_scaled, dk_far, dv_far, dk_near, dv_near, dk_low, dv_low,
    inverse, key_at, usable, query_of, pair_of, sent, got, halo_sent, halo_got,
):
    me = Place()
    has_before, has_after = me.slice > 0, me.slice < me.last
    greet(me)

    arrivals = ((k_in, kx, SP), (v_in, vx, SP), (q_in, q, 0), (g_in, g, 0))
    for a, (src, dst, first) in enumerate(arrivals):

        def push(n):
            h = me.nth_head(n)
            target = me.worker_of_mine(h)
            to = half_rows(dst, me.mine, first)

            @pl.when(jnp.logical_not(me.is_me(target)))
            def _():
                send(head_columns(src, h), to, sent.at[a, h], got.at[a, me.mine], target)

            @pl.when(me.is_me(target))
            def _():
                pltpu.make_async_copy(head_columns(src, h), to, got.at[a, me.mine]).start()

        loop(HEADS, push)

    tables(me, windows, tile_place, inverse, key_at, usable, query_of, pair_of)
    probs[NONE] = jnp.zeros((TILE, TILE), BF)
    dscores[NONE] = jnp.zeros((TILE, TILE), BF)

    def exchange(a, to_before, to_after, from_before, from_after):
        @pl.when(has_before)
        def _():
            send(to_before, from_after, halo_sent.at[a, 0], halo_got.at[a, 1], me.before())

        @pl.when(has_after)
        def _():
            send(to_after, from_before, halo_sent.at[a, 1], halo_got.at[a, 0], me.after())

    def exchanged(a, to_before, to_after, from_before, from_after):
        @pl.when(has_before)
        def _():
            landed(from_before, halo_got.at[a, 0])
            landed(to_before, halo_sent.at[a, 0])

        @pl.when(has_after)
        def _():
            landed(from_after, halo_got.at[a, 1])
            landed(to_after, halo_sent.at[a, 1])

    def key_halo(x):
        own = x.at[pl.ds(SP, SP)]
        return own, own, x.at[pl.ds(0, SP)], x.at[pl.ds(2 * SP, SP)]

    def grad_halo(far, near):
        first, second = pl.ds(0, SP), pl.ds(SP, SP)
        return far.at[first], far.at[second], near.at[first], near.at[second]

    for a, x in enumerate((kx, vx)):
        loop(HEADS, lambda i: landed(half_rows(x, i, SP), got.at[a, i]))
        exchange(a, *key_halo(x))
    for a, x in enumerate((kx, vx)):
        exchanged(a, *key_halo(x))

    def push_back(a, src, dst, i):
        target = me.holder(i)
        to = head_columns(dst, me.head)

        @pl.when(jnp.logical_not(me.is_me(target)))
        def _():
            send(half_rows(src, i), to, sent.at[a, i], got.at[a, me.head], target)

        @pl.when(me.is_me(target))
        def _():
            pltpu.make_async_copy(half_rows(src, i), to, got.at[a, me.head]).start()

    def query_step(i):
        for part in (2 * i, 2 * i + 1):
            landed(half_rows(q, part), got.at[2, part])
            landed(half_rows(g, part), got.at[3, part])
        query_tile(i, key_at, usable, q, g, kx, vx, o, dq, probs, dscores, q_scaled, g_scaled)
        for part in (2 * i, 2 * i + 1):
            push_back(4, o, o_out, part)
            push_back(5, dq, dq_out, part)

    loop(SP, query_step)

    def far_step(n):
        m = jnp.where(n < SP, n, n + SP)
        grad_k, grad_v = key_tile(m, query_of, pair_of, q_scaled, g_scaled, probs, dscores)
        dk_far[n] = grad_k.astype(BF)
        dv_far[n] = grad_v.astype(BF)

    loop(2 * SP, far_step)
    halos = (grad_halo(dk_far, dk_near), grad_halo(dv_far, dv_near))
    for a, halo in enumerate(halos):
        exchange(2 + a, *halo)

    @pl.when(jnp.logical_not(has_before))
    def _():
        for near in (dk_near, dv_near):
            near[pl.ds(0, SP)] = jnp.zeros((SP, TILE, HD), BF)

    @pl.when(jnp.logical_not(has_after))
    def _():
        for near in (dk_near, dv_near):
            near[pl.ds(SP, SP)] = jnp.zeros((SP, TILE, HD), BF)

    for a, halo in enumerate(halos):
        exchanged(2 + a, *halo)

    def own_step(m):
        grad_k, grad_v = key_tile(SP + m, query_of, pair_of, q_scaled, g_scaled, probs, dscores)
        dk_low[m] = (grad_k + dk_near[m].astype(F32) + dk_near[SP + m].astype(F32)).astype(BF)
        dv_low[m] = (grad_v + dv_near[m].astype(F32) + dv_near[SP + m].astype(F32)).astype(BF)
        for part in (2 * m, 2 * m + 1):
            push_back(6, dk_low, dk_out, part)
            push_back(7, dv_low, dv_out, part)

    loop(SP, own_step)

    for a, (_, dst, first) in enumerate(arrivals):

        def drain(n):
            @pl.when(jnp.logical_not(me.is_me(me.worker_of_mine(n))))
            def _():
                landed(half_rows(dst, me.mine, first), sent.at[a, n])

        loop(HEADS, drain)

    for a, (src, dst) in enumerate(((o, o_out), (dq, dq_out), (dk_low, dk_out), (dv_low, dv_out))):

        def finish(i):
            landed(head_columns(dst, i), got.at[4 + a, i])

            @pl.when(jnp.logical_not(me.is_me(me.holder(i))))
            def _():
                landed(half_rows(src, i), sent.at[4 + a, i])

        loop(HEADS, finish)


def body(queries, key_rows, value_rows, grad_out, windows, tile_place):
    anywhere = pl.BlockSpec(memory_space=pl.ANY)
    smem = pl.BlockSpec(memory_space=pltpu.SMEM)
    tiles = lambda n: pltpu.VMEM((n, TILE, HD), BF)
    pairs = pltpu.VMEM((NONE + 1, TILE, TILE), BF)
    numbers = lambda n: pltpu.SMEM((n,), jnp.int32)
    dma = pltpu.SemaphoreType.DMA
    rows = jax.ShapeDtypeStruct(queries.shape, BF)
    return pl.pallas_call(
        attention_kernel,
        out_shape=[rows] * 4,
        in_specs=[smem] * 2 + [anywhere] * 4,
        out_specs=[anywhere] * 4,
        scratch_shapes=[tiles(SP), tiles(3 * SP), tiles(3 * SP), tiles(SP), tiles(SP), tiles(SP), pairs, pairs]
        + [tiles(SP)] * 2
        + [tiles(2 * SP)] * 4
        + [tiles(SP)] * 2
        + [numbers(3 * SP), numbers(SP * W), numbers(SP * W), numbers(9 * SP), numbers(9 * SP)]
        + [dma((8, HEADS)), dma((8, HEADS)), dma((4, 2)), dma((4, 2))],
        compiler_params=pltpu.CompilerParams(
            collective_id=0, has_side_effects=True, vmem_limit_bytes=56 * 1024 * 1024
        ),
        name="attention",
    )(windows, tile_place, queries, key_rows, value_rows, grad_out)


def solution(mesh):
    spread = P(("tm", "head"), None)
    return jax.shard_map(
        body,
        mesh=mesh,
        in_specs=(spread,) * 4 + (P(), P()),
        out_specs=(spread,) * 4,
        check_vma=False,
    )
```

```python
import functools

import jax
import jax.numpy as jnp
import numpy as np
from jax import lax
from jax.sharding import PartitionSpec as P
import jax.experimental.pallas as pl
import jax.experimental.pallas.tpu as pltpu

HD = 128
HEADS = 16
TILE = 256
SP = 8
W = 6
HALF = 128
NONE = SP * W
MESH = pl.DeviceIdType.MESH
BF = jnp.bfloat16
F32 = jnp.float32
SCALE = HD**-0.5
SCALE2 = float(SCALE * np.log2(np.e))
NN = (((1,), (0,)), ((), ()))
TN = (((0,), (0,)), ((), ()))


def dot(a, b, dims):
    return lax.dot_general(a, b, dims, preferred_element_type=F32)


class Place:
    def __init__(self):
        self.tm = lax.axis_index("tm")
        self.index = lax.axis_index("head")
        self.low, self.y = self.tm // 4, lax.rem(self.tm, 4)
        self.x = x = self.index // 8
        self.z = z = 2 * lax.rem(self.index // 2, 4) + self.low
        self.half, self.mine = self.index // HEADS, lax.rem(self.index, HEADS)
        self.core = lax.rem(self.index, 2)
        self.head = 8 * (x // 2) + z
        self.group = 4 * lax.rem(x + z, 2) + self.y
        self.slice = 2 * self.group + self.core
        self.last = 2 * lax.axis_size("tm") - 1
        self.stays = (self.group == self.tm) & (self.core == self.half)

    def worker(self, group, head, core):
        z = lax.rem(head, 8)
        x = 2 * (head // 8) + lax.rem(group // 4 + z, 2)
        return 4 * lax.rem(z, 2) + lax.rem(group, 4), 8 * x + 2 * (z // 2) + core

    def worker_of_mine(self, head):
        return self.worker(self.tm, head, self.half)

    def holder(self, i):
        return self.group, HEADS * self.core + i

    def is_me(self, device):
        return (device[0] == self.tm) & (device[1] == self.index)

    def nth_head(self, n):
        step = n // 2
        far = (step + 1) // 2
        turn = jnp.where(lax.rem(step, 2) == 1, far, 8 - far)
        return 8 * lax.rem(self.head // 8 + n, 2) + lax.rem(self.head + turn, 8)

    def nth_tile(self, n):
        step = n // 2
        even = lax.rem(self.z + self.group // 4, 2) == 0
        near = jnp.where(even, jnp.where(step == 1, 2, 0), jnp.where(step == 1, 7, 1))
        far = jnp.where(even, jnp.where(step == 2, 6, 4), jnp.where(step == 2, 3, 5))
        z = lax.rem(self.z + jnp.where(step < 2, near, far), 8)
        return 4 * lax.rem(self.x + n, 2) + z // 2

    def before(self):
        return self.worker(self.group - 1 + self.core, self.head, 1 - self.core)

    def after(self):
        return self.worker(self.group + self.core, self.head, 1 - self.core)


def greet(me):
    barrier = pltpu.get_barrier_semaphore()

    def signal(i):
        for other in (me.worker_of_mine(i), me.holder(i)):

            @pl.when(jnp.logical_not(me.is_me(other)))
            def _():
                pl.semaphore_signal(barrier, 1, device_id=other, device_id_type=MESH)

    loop(HEADS, signal)
    has_before, has_after = me.slice > 0, me.slice < me.last

    @pl.when(has_before)
    def _():
        pl.semaphore_signal(barrier, 1, device_id=me.before(), device_id_type=MESH)

    @pl.when(has_after)
    def _():
        pl.semaphore_signal(barrier, 1, device_id=me.after(), device_id_type=MESH)

    own = jnp.where(me.stays, 2, 0)
    pl.semaphore_wait(barrier, 2 * HEADS - own + has_before.astype(jnp.int32) + has_after.astype(jnp.int32))


def landed(ref, sem):
    pltpu.make_async_copy(ref, ref, sem).wait()


def send(src, dst, send_sem, recv_sem, target):
    pltpu.make_async_remote_copy(
        src_ref=src, dst_ref=dst, send_sem=send_sem, recv_sem=recv_sem, device_id=target, device_id_type=MESH
    ).start()


def half_rows(ref, i, first=0):
    return ref.at[first + i // 2, pl.ds(pl.multiple_of(lax.rem(i, 2) * HALF, HALF), HALF)]


def head_columns(ref, h):
    return ref.at[:, pl.ds(pl.multiple_of(h * HD, HD), HD)]


def loop(n, step):
    def body(i, carry):
        step(i)
        return carry

    lax.fori_loop(0, n, body, 0)


def tables(me, windows, tile_place, inverse, key_at, usable, query_of, pair_of):
    slice_id, last = me.slice, me.last

    def invert(n):
        near = jnp.clip(slice_id - 1 + n // SP, 0, last)
        tile = lax.rem(n, SP)
        found = jnp.int32(0)
        for i in range(SP):
            found = jnp.where(tile_place[i, near] == tile, i, found)
        inverse[n] = found

    loop(3 * SP, invert)

    def query(n):
        i = n // W
        w = lax.rem(n, W)
        tile = SP * slice_id + jnp.clip(tile_place[i, slice_id], 0, SP - 1)
        listed = windows[w, tile]
        good = listed >= 0
        named = jnp.where(good, listed, windows[2, tile])
        near = jnp.clip(named - SP * (slice_id - 1), 0, 3 * SP - 1)
        key_at[n] = inverse[near] + SP * jnp.where(good, w // 2, 1)
        usable[n] = good.astype(jnp.int32)

    loop(SP * W, query)

    def key(n):
        m = n // 3
        j = m // SP
        near = jnp.clip(slice_id - 1 + j, 0, last)
        tile = jnp.clip(tile_place[lax.rem(m, SP), near], 0, SP - 1)
        row = tile // 2 + lax.rem(n, 3) - 1
        inside = (row >= 0) & (row < SP // 2)
        asker = jnp.where(inside, 2 * row + lax.rem(tile, 2), 0)
        i = inverse[SP + asker]
        name = SP * near + tile
        first = windows[2 * j, SP * slice_id + asker] == name
        second = windows[2 * j + 1, SP * slice_id + asker] == name
        query_of[n] = i
        pair_of[n] = jnp.where(
            inside & (first | second), i * W + 2 * j + jnp.where(second, 1, 0), NONE
        )

    loop(9 * SP, key)


def forward_tile(i, key_at, usable, q, kx, vx, o, o_turned, share, probs, q_scaled):
    q_rows = q[i]
    q_turned = q_rows.T
    at = [key_at[i * W + w] for w in range(W)]
    scores = [dot(kx[at[w]], q_turned, NN) for w in range(W)]
    peak = scores[0]
    for w in range(1, W):
        peak = jnp.maximum(peak, scores[w])
    peak = jnp.max(peak, axis=0, keepdims=True) * SCALE2
    total = jnp.zeros((1, TILE), F32)
    out = jnp.zeros((HD, TILE), F32)
    for w in range(W):
        level = peak + jnp.where(usable[i * W + w] > 0, 0.0, 1e30)
        e = jnp.exp2(scores[w] * SCALE2 - level)
        total = total + jnp.sum(e, axis=0, keepdims=True)
        low = e.astype(BF)
        probs[i * W + w] = low
        out = out + dot(vx[at[w]], low, TN)
    part = 1.0 / total
    out_low = (out * part).astype(BF)
    share[i] = part
    o_turned[i] = out_low
    o[i] = out_low.T
    part_rows = jnp.transpose(jnp.broadcast_to(part, (HD, TILE)))
    q_scaled[i] = (q_rows.astype(F32) * (part_rows * SCALE)).astype(BF)


def backward_tile(i, key_at, g, kx, vx, dq, o_turned, share, probs, dscores, g_scaled):
    g_rows = g[i]
    g_turned = g_rows.T
    at = [key_at[i * W + w] for w in range(W)]
    part = share[i]
    row_term = jnp.sum(g_turned.astype(F32) * o_turned[i].astype(F32), axis=0, keepdims=True)
    grad = jnp.zeros((HD, TILE), F32)
    for w in range(W):
        dprobs = dot(vx[at[w]], g_turned, NN)
        low = (probs[i * W + w].astype(F32) * (dprobs - row_term)).astype(BF)
        dscores[i * W + w] = low
        grad = grad + dot(kx[at[w]], low, TN)
    dq[i] = (grad * (part * SCALE)).astype(BF).T
    part_rows = jnp.transpose(jnp.broadcast_to(part, (HD, TILE)))
    g_scaled[i] = (g_rows.astype(F32) * part_rows).astype(BF)


def key_tile(m, query_of, pair_of, q_scaled, g_scaled, probs, dscores):
    grad_k = jnp.zeros((TILE, HD), F32)
    grad_v = jnp.zeros((TILE, HD), F32)
    for n in range(3):
        i = query_of[3 * m + n]
        pair = pair_of[3 * m + n]
        grad_v = grad_v + dot(probs[pair], g_scaled[i], NN)
        grad_k = grad_k + dot(dscores[pair], q_scaled[i], NN)
    return grad_k, grad_v


def attention_kernel(
    windows, tile_place, q_in, k_in, v_in, g_in, o_out, dq_out, dk_out, dv_out,
    q, kx, vx, g, o, dq, o_turned, share, probs, dscores, q_scaled, g_scaled, dk_far, dv_far, dk_near, dv_near,
    dk_low, dv_low, inverse, key_at, usable, query_of, pair_of, sent, got, halo_sent, halo_got, grad_sent, grad_got,
):
    me = Place()
    has_before, has_after = me.slice > 0, me.slice < me.last
    greet(me)

    arrivals = ((k_in, kx, SP), (v_in, vx, SP), (q_in, q, 0), (g_in, g, 0))
    def push_all(a):
        src, dst, first = arrivals[a]

        def push(n):
            h = me.nth_head(n)
            target = me.worker_of_mine(h)
            to = half_rows(dst, me.mine, first)

            @pl.when(jnp.logical_not(me.is_me(target)))
            def _():
                send(head_columns(src, h), to, sent.at[a, h], got.at[a, me.mine], target)

            @pl.when(me.is_me(target))
            def _():
                pltpu.make_async_copy(head_columns(src, h), to, got.at[a, me.mine]).start()

        loop(HEADS, push)

    for a in (0, 1, 2, 3):
        push_all(a)
    tables(me, windows, tile_place, inverse, key_at, usable, query_of, pair_of)
    probs[NONE] = jnp.zeros((TILE, TILE), BF)
    dscores[NONE] = jnp.zeros((TILE, TILE), BF)

    def exchange(a, to_before, to_after, from_before, from_after):
        @pl.when(has_before)
        def _():
            send(to_before, from_after, halo_sent.at[a, 0], halo_got.at[a, 1], me.before())

        @pl.when(has_after)
        def _():
            send(to_after, from_before, halo_sent.at[a, 1], halo_got.at[a, 0], me.after())

    def exchanged(a, to_before, to_after, from_before, from_after):
        @pl.when(has_before)
        def _():
            landed(from_before, halo_got.at[a, 0])
            landed(to_before, halo_sent.at[a, 0])

        @pl.when(has_after)
        def _():
            landed(from_after, halo_got.at[a, 1])
            landed(to_after, halo_sent.at[a, 1])

    def key_halo(x):
        own = x.at[pl.ds(SP, SP)]
        return own, own, x.at[pl.ds(0, SP)], x.at[pl.ds(2 * SP, SP)]

    def arrived(a):
        _, dst, first = arrivals[a]
        loop(HEADS, lambda i: landed(half_rows(dst, i, first), got.at[a, i]))

    for a, x in enumerate((kx, vx)):
        arrived(a)
        exchange(a, *key_halo(x))
    for a, x in enumerate((kx, vx)):
        exchanged(a, *key_halo(x))
    def push_back(a, src, dst, i):
        target = me.holder(i)
        to = head_columns(dst, me.head)

        @pl.when(jnp.logical_not(me.is_me(target)))
        def _():
            send(half_rows(src, i), to, sent.at[a, i], got.at[a, me.head], target)

        @pl.when(me.is_me(target))
        def _():
            pltpu.make_async_copy(half_rows(src, i), to, got.at[a, me.head]).start()

    def forward_step(n):
        i = me.nth_tile(n)
        for part in (2 * i, 2 * i + 1):
            landed(half_rows(q, part), got.at[2, part])
        forward_tile(i, key_at, usable, q, kx, vx, o, o_turned, share, probs, q_scaled)
        for part in (2 * i, 2 * i + 1):
            push_back(4, o, o_out, part)

    def backward_step(n):
        i = me.nth_tile(n)
        for part in (2 * i, 2 * i + 1):
            landed(half_rows(g, part), got.at[3, part])
        backward_tile(i, key_at, g, kx, vx, dq, o_turned, share, probs, dscores, g_scaled)
        for part in (2 * i, 2 * i + 1):
            push_back(5, dq, dq_out, part)

    loop(SP, forward_step)
    loop(SP, backward_step)

    def far_step(k):
        n = lax.rem(k + SP * me.core, 2 * SP)
        m = jnp.where(n < SP, n, n + SP)
        grad_k, grad_v = key_tile(m, query_of, pair_of, q_scaled, g_scaled, probs, dscores)
        dk_far[n] = grad_k.astype(BF)
        dv_far[n] = grad_v.astype(BF)
        there = lax.rem(n + SP, 2 * SP)
        for a, (far, near) in enumerate(grads):

            @pl.when((n < SP) & has_before)
            def _():
                send(far.at[n], near.at[there], grad_sent.at[a, n], grad_got.at[a, there], me.before())

            @pl.when((n >= SP) & has_after)
            def _():
                send(far.at[n], near.at[there], grad_sent.at[a, n], grad_got.at[a, there], me.after())

    grads = ((dk_far, dk_near), (dv_far, dv_near))
    loop(2 * SP, far_step)

    @pl.when(jnp.logical_not(has_before))
    def _():
        for near in (dk_near, dv_near):
            near[pl.ds(0, SP)] = jnp.zeros((SP, TILE, HD), BF)

    @pl.when(jnp.logical_not(has_after))
    def _():
        for near in (dk_near, dv_near):
            near[pl.ds(SP, SP)] = jnp.zeros((SP, TILE, HD), BF)

    def own_step(n):
        m = me.nth_tile(n)
        grad_k, grad_v = key_tile(SP + m, query_of, pair_of, q_scaled, g_scaled, probs, dscores)
        for a, (_, near) in enumerate(grads):

            @pl.when(has_before)
            def _():
                landed(near.at[m], grad_got.at[a, m])

            @pl.when(has_after)
            def _():
                landed(near.at[SP + m], grad_got.at[a, SP + m])

        dk_low[m] = (grad_k + dk_near[m].astype(F32) + dk_near[SP + m].astype(F32)).astype(BF)
        dv_low[m] = (grad_v + dv_near[m].astype(F32) + dv_near[SP + m].astype(F32)).astype(BF)
        for part in (2 * m, 2 * m + 1):
            push_back(6, dk_low, dk_out, part)
            push_back(7, dv_low, dv_out, part)

    loop(SP, own_step)

    def drain_far(n):
        for a, (far, _) in enumerate(grads):

            @pl.when(jnp.where(n < SP, has_before, has_after))
            def _():
                landed(far.at[n], grad_sent.at[a, n])

    loop(2 * SP, drain_far)

    for a, (_, dst, first) in enumerate(arrivals):

        def drain(n):
            @pl.when(jnp.logical_not(me.is_me(me.worker_of_mine(n))))
            def _():
                landed(half_rows(dst, me.mine, first), sent.at[a, n])

        loop(HEADS, drain)

    for a, (src, dst) in enumerate(((o, o_out), (dq, dq_out), (dk_low, dk_out), (dv_low, dv_out))):

        def finish(i):
            landed(head_columns(dst, i), got.at[4 + a, i])

            @pl.when(jnp.logical_not(me.is_me(me.holder(i))))
            def _():
                landed(half_rows(src, i), sent.at[4 + a, i])

        loop(HEADS, finish)


def write_kernel(*refs):
    sources, targets, held, sems = refs[:4], refs[4:8], refs[8:12], refs[12]
    reads = [pltpu.make_async_copy(src, mid, sems.at[0, n]) for n, (src, mid) in enumerate(zip(sources, held))]
    writes = [pltpu.make_async_copy(mid, dst, sems.at[1, n]) for n, (mid, dst) in enumerate(zip(held, targets))]
    for read in reads:
        read.start()
    for read, write in zip(reads, writes):
        read.wait()
        write.start()
    for write in writes:
        write.wait()


def body(queries, key_rows, value_rows, grad_out, windows, tile_place):
    anywhere = pl.BlockSpec(memory_space=pl.ANY)
    smem = pl.BlockSpec(memory_space=pltpu.SMEM)
    tiles = lambda n: pltpu.VMEM((n, TILE, HD), BF)
    pairs = pltpu.VMEM((NONE + 1, TILE, TILE), BF)
    numbers = lambda n: pltpu.SMEM((n,), jnp.int32)
    dma = pltpu.SemaphoreType.DMA
    rows = jax.ShapeDtypeStruct(queries.shape, BF)
    results = pl.pallas_call(
        attention_kernel,
        out_shape=[rows] * 4,
        in_specs=[smem] * 2 + [anywhere] * 4,
        out_specs=[anywhere] * 4,
        scratch_shapes=[tiles(SP), tiles(3 * SP), tiles(3 * SP), tiles(SP), tiles(SP), tiles(SP)]
        + [pltpu.VMEM((SP, HD, TILE), BF), pltpu.VMEM((SP, 1, TILE), F32), pairs, pairs]
        + [tiles(SP)] * 2
        + [tiles(2 * SP)] * 4
        + [tiles(SP)] * 2
        + [numbers(3 * SP), numbers(SP * W), numbers(SP * W), numbers(9 * SP), numbers(9 * SP)]
        + [dma((8, HEADS)), dma((8, HEADS)), dma((2, 2)), dma((2, 2)), dma((2, 2 * SP)), dma((2, 2 * SP))],
        compiler_params=pltpu.CompilerParams(
            collective_id=0, has_side_effects=True, vmem_limit_bytes=56 * 1024 * 1024
        ),
        name="attention",
    )(windows.T, tile_place.T, queries, key_rows, value_rows, grad_out)
    return pl.pallas_call(
        write_kernel,
        out_shape=[rows] * 4,
        in_specs=[anywhere] * 4,
        out_specs=[anywhere] * 4,
        scratch_shapes=[pltpu.VMEM(queries.shape, BF)] * 4 + [dma((2, 4))],
        name="write",
    )(*results)


def solution(mesh):
    spread = P(("tm", "head"), None)
    return jax.shard_map(
        body,
        mesh=mesh,
        in_specs=(spread,) * 4 + (P(), P()),
        out_specs=(spread,) * 4,
        check_vma=False,
    )
```

```python
import functools

import jax
import jax.numpy as jnp
import numpy as np
from jax import lax
from jax.sharding import PartitionSpec as P
import jax.experimental.pallas as pl
import jax.experimental.pallas.tpu as pltpu

HD = 128
HEADS = 16
TILE = 256
SP = 8
W = 6
HALF = 128
NONE = SP * W
MESH = pl.DeviceIdType.MESH
BF = jnp.bfloat16
F32 = jnp.float32
SCALE = HD**-0.5
SCALE2 = float(SCALE * np.log2(np.e))
NN = (((1,), (0,)), ((), ()))
TN = (((0,), (0,)), ((), ()))


def dot(a, b, dims):
    return lax.dot_general(a, b, dims, preferred_element_type=F32)


class Place:
    def __init__(self):
        self.tm = lax.axis_index("tm")
        self.index = lax.axis_index("head")
        self.low, self.y = self.tm // 4, lax.rem(self.tm, 4)
        self.x = x = self.index // 8
        self.z = z = 2 * lax.rem(self.index // 2, 4) + self.low
        self.half, self.mine = self.index // HEADS, lax.rem(self.index, HEADS)
        self.core = lax.rem(self.index, 2)
        self.head = 8 * (x // 2) + z
        self.group = 4 * lax.rem(x + z, 2) + self.y
        self.slice = 2 * self.group + self.core
        self.last = 2 * lax.axis_size("tm") - 1
        self.stays = (self.group == self.tm) & (self.core == self.half)

    def worker(self, group, head, core):
        z = lax.rem(head, 8)
        x = 2 * (head // 8) + lax.rem(group // 4 + z, 2)
        return 4 * lax.rem(z, 2) + lax.rem(group, 4), 8 * x + 2 * (z // 2) + core

    def worker_of_mine(self, head):
        return self.worker(self.tm, head, self.half)

    def holder(self, i):
        return self.group, HEADS * self.core + i

    def is_me(self, device):
        return (device[0] == self.tm) & (device[1] == self.index)

    def nth_head(self, n):
        step = n // 2
        far = (step + 1) // 2
        turn = jnp.where(lax.rem(step, 2) == 1, far, 8 - far)
        return 8 * lax.rem(self.head // 8 + n, 2) + lax.rem(self.head + turn, 8)

    def nth_tile(self, n):
        step = n // 2
        even = lax.rem(self.z + self.group // 4, 2) == 0
        near = jnp.where(even, jnp.where(step == 1, 2, 0), jnp.where(step == 1, 7, 1))
        far = jnp.where(even, jnp.where(step == 2, 6, 4), jnp.where(step == 2, 3, 5))
        z = lax.rem(self.z + jnp.where(step < 2, near, far), 8)
        return 4 * lax.rem(self.x + n, 2) + z // 2

    def before(self):
        return self.worker(self.group - 1 + self.core, self.head, 1 - self.core)

    def after(self):
        return self.worker(self.group + self.core, self.head, 1 - self.core)


def greet(me):
    barrier = pltpu.get_barrier_semaphore()

    def signal(i):
        for other in (me.worker_of_mine(i), me.holder(i)):

            @pl.when(jnp.logical_not(me.is_me(other)))
            def _():
                pl.semaphore_signal(barrier, 1, device_id=other, device_id_type=MESH)

    loop(HEADS, signal)
    has_before, has_after = me.slice > 0, me.slice < me.last

    @pl.when(has_before)
    def _():
        pl.semaphore_signal(barrier, 1, device_id=me.before(), device_id_type=MESH)

    @pl.when(has_after)
    def _():
        pl.semaphore_signal(barrier, 1, device_id=me.after(), device_id_type=MESH)

    own = jnp.where(me.stays, 2, 0)
    pl.semaphore_wait(barrier, 2 * HEADS - own + has_before.astype(jnp.int32) + has_after.astype(jnp.int32))


def landed(ref, sem):
    pltpu.make_async_copy(ref, ref, sem).wait()


def send(src, dst, send_sem, recv_sem, target):
    pltpu.make_async_remote_copy(
        src_ref=src, dst_ref=dst, send_sem=send_sem, recv_sem=recv_sem, device_id=target, device_id_type=MESH
    ).start()


def half_rows(ref, i, first=0):
    return ref.at[first + i // 2, pl.ds(pl.multiple_of(lax.rem(i, 2) * HALF, HALF), HALF)]


def head_columns(ref, h):
    return ref.at[:, pl.ds(pl.multiple_of(h * HD, HD), HD)]


def loop(n, step):
    def body(i, carry):
        step(i)
        return carry

    lax.fori_loop(0, n, body, 0)


def tables(me, windows, tile_place, inverse, key_at, usable, query_of, pair_of):
    slice_id, last = me.slice, me.last

    def invert(n):
        near = jnp.clip(slice_id - 1 + n // SP, 0, last)
        tile = lax.rem(n, SP)
        found = jnp.int32(0)
        for i in range(SP):
            found = jnp.where(tile_place[i, near] == tile, i, found)
        inverse[n] = found

    loop(3 * SP, invert)

    def query(n):
        i = n // W
        w = lax.rem(n, W)
        tile = SP * slice_id + jnp.clip(tile_place[i, slice_id], 0, SP - 1)
        listed = windows[w, tile]
        good = listed >= 0
        named = jnp.where(good, listed, windows[2, tile])
        near = jnp.clip(named - SP * (slice_id - 1), 0, 3 * SP - 1)
        key_at[n] = inverse[near] + SP * jnp.where(good, w // 2, 1)
        usable[n] = good.astype(jnp.int32)

    loop(SP * W, query)

    def key(n):
        m = n // 3
        j = m // SP
        near = jnp.clip(slice_id - 1 + j, 0, last)
        tile = jnp.clip(tile_place[lax.rem(m, SP), near], 0, SP - 1)
        row = tile // 2 + lax.rem(n, 3) - 1
        inside = (row >= 0) & (row < SP // 2)
        asker = jnp.where(inside, 2 * row + lax.rem(tile, 2), 0)
        i = inverse[SP + asker]
        name = SP * near + tile
        first = windows[2 * j, SP * slice_id + asker] == name
        second = windows[2 * j + 1, SP * slice_id + asker] == name
        query_of[n] = i
        pair_of[n] = jnp.where(
            inside & (first | second), i * W + 2 * j + jnp.where(second, 1, 0), NONE
        )

    loop(9 * SP, key)


def forward_tile(i, key_at, usable, q, kx, vx, o, o_turned, share, probs, q_scaled):
    q_rows = q[i]
    q_turned = q_rows.T
    at = [key_at[i * W + w] for w in range(W)]
    scores = [dot(kx[at[w]], q_turned, NN) for w in range(W)]
    peak = scores[0]
    for w in range(1, W):
        peak = jnp.maximum(peak, scores[w])
    peak = jnp.max(peak, axis=0, keepdims=True) * SCALE2
    total = jnp.zeros((1, TILE), F32)
    out = jnp.zeros((HD, TILE), F32)
    for w in range(W):
        level = peak + jnp.where(usable[i * W + w] > 0, 0.0, 1e30)
        e = jnp.exp2(scores[w] * SCALE2 - level)
        total = total + jnp.sum(e, axis=0, keepdims=True)
        low = e.astype(BF)
        probs[i * W + w] = low
        out = out + dot(vx[at[w]], low, TN)
    part = 1.0 / total
    out_low = (out * part).astype(BF)
    share[i] = part
    o_turned[i] = out_low
    o[i] = out_low.T
    part_rows = jnp.transpose(jnp.broadcast_to(part, (HD, TILE)))
    q_scaled[i] = (q_rows.astype(F32) * (part_rows * SCALE)).astype(BF)


def backward_tile(i, key_at, g, kx, vx, dq, o_turned, share, probs, dscores, g_scaled):
    g_rows = g[i]
    g_turned = g_rows.T
    at = [key_at[i * W + w] for w in range(W)]
    part = share[i]
    row_term = jnp.sum(g_turned.astype(F32) * o_turned[i].astype(F32), axis=0, keepdims=True)
    grad = jnp.zeros((HD, TILE), F32)
    for w in range(W):
        dprobs = dot(vx[at[w]], g_turned, NN)
        low = (probs[i * W + w].astype(F32) * (dprobs - row_term)).astype(BF)
        dscores[i * W + w] = low
        grad = grad + dot(kx[at[w]], low, TN)
    dq[i] = (grad * (part * SCALE)).astype(BF).T
    part_rows = jnp.transpose(jnp.broadcast_to(part, (HD, TILE)))
    g_scaled[i] = (g_rows.astype(F32) * part_rows).astype(BF)


def key_tile(m, query_of, pair_of, q_scaled, g_scaled, probs, dscores):
    grad_k = jnp.zeros((TILE, HD), F32)
    grad_v = jnp.zeros((TILE, HD), F32)
    for n in range(3):
        i = query_of[3 * m + n]
        pair = pair_of[3 * m + n]
        grad_v = grad_v + dot(probs[pair], g_scaled[i], NN)
        grad_k = grad_k + dot(dscores[pair], q_scaled[i], NN)
    return grad_k, grad_v


def attention_kernel(
    windows, tile_place, q_in, k_in, v_in, g_in, o_out, dq_out, dk_out, dv_out,
    q, kx, vx, g, o, dq, o_turned, share, probs, dscores, q_scaled, g_scaled, dk_far, dv_far, dk_near, dv_near,
    dk_low, dv_low, inverse, key_at, usable, query_of, pair_of, sent, got, halo_sent, halo_got, grad_sent, grad_got,
):
    me = Place()
    has_before, has_after = me.slice > 0, me.slice < me.last
    greet(me)

    arrivals = ((k_in, kx, SP), (v_in, vx, SP), (q_in, q, 0), (g_in, g, 0))
    def push_all(a):
        src, dst, first = arrivals[a]

        def push(n):
            h = me.nth_head(HEADS - 1 - n)
            target = me.worker_of_mine(h)
            to = half_rows(dst, me.mine, first)

            @pl.when(jnp.logical_not(me.is_me(target)))
            def _():
                send(head_columns(src, h), to, sent.at[a, h], got.at[a, me.mine], target)

            @pl.when(me.is_me(target))
            def _():
                pltpu.make_async_copy(head_columns(src, h), to, got.at[a, me.mine]).start()

        loop(HEADS, push)

    for a in (0, 1, 2, 3):
        push_all(a)
    tables(me, windows, tile_place, inverse, key_at, usable, query_of, pair_of)
    probs[NONE] = jnp.zeros((TILE, TILE), BF)
    dscores[NONE] = jnp.zeros((TILE, TILE), BF)

    def pass_on(a, n):
        src, x, first = arrivals[a]
        i = me.nth_tile(SP - 1 - n)
        for part in (2 * i, 2 * i + 1):
            landed(half_rows(x, part, SP), got.at[a, part])

        @pl.when(has_before)
        def _():
            send(x.at[SP + i], x.at[2 * SP + i], halo_sent.at[a, i], halo_got.at[a, SP + i], me.before())

        @pl.when(has_after)
        def _():
            send(x.at[SP + i], x.at[i], halo_sent.at[a, SP + i], halo_got.at[a, i], me.after())

    def passed_on(a, i):
        x = arrivals[a][1]

        @pl.when(has_before)
        def _():
            landed(x.at[i], halo_got.at[a, i])
            landed(x.at[SP + i], halo_sent.at[a, i])

        @pl.when(has_after)
        def _():
            landed(x.at[2 * SP + i], halo_got.at[a, SP + i])
            landed(x.at[SP + i], halo_sent.at[a, SP + i])

    for a in (0, 1):
        loop(SP, functools.partial(pass_on, a))
    for a in (0, 1):
        loop(SP, functools.partial(passed_on, a))

    def push_back(a, src, dst, i):
        target = me.holder(i)
        to = head_columns(dst, me.head)

        @pl.when(jnp.logical_not(me.is_me(target)))
        def _():
            send(half_rows(src, i), to, sent.at[a, i], got.at[a, me.head], target)

        @pl.when(me.is_me(target))
        def _():
            pltpu.make_async_copy(half_rows(src, i), to, got.at[a, me.head]).start()

    def forward_step(n):
        i = me.nth_tile(SP - 1 - n)
        for part in (2 * i, 2 * i + 1):
            landed(half_rows(q, part), got.at[2, part])
        forward_tile(i, key_at, usable, q, kx, vx, o, o_turned, share, probs, q_scaled)
        for part in (2 * i, 2 * i + 1):
            push_back(4, o, o_out, part)

    def backward_step(n):
        i = me.nth_tile(SP - 1 - n)
        for part in (2 * i, 2 * i + 1):
            landed(half_rows(g, part), got.at[3, part])
        backward_tile(i, key_at, g, kx, vx, dq, o_turned, share, probs, dscores, g_scaled)
        for part in (2 * i, 2 * i + 1):
            push_back(5, dq, dq_out, part)

    loop(SP, forward_step)
    loop(SP, backward_step)

    def far_step(k):
        n = lax.rem(k + SP * me.core, 2 * SP)
        m = jnp.where(n < SP, n, n + SP)
        grad_k, grad_v = key_tile(m, query_of, pair_of, q_scaled, g_scaled, probs, dscores)
        dk_far[n] = grad_k.astype(BF)
        dv_far[n] = grad_v.astype(BF)
        there = lax.rem(n + SP, 2 * SP)
        for a, (far, near) in enumerate(grads):

            @pl.when((n < SP) & has_before)
            def _():
                send(far.at[n], near.at[there], grad_sent.at[a, n], grad_got.at[a, there], me.before())

            @pl.when((n >= SP) & has_after)
            def _():
                send(far.at[n], near.at[there], grad_sent.at[a, n], grad_got.at[a, there], me.after())

    grads = ((dk_far, dk_near), (dv_far, dv_near))
    loop(2 * SP, far_step)

    @pl.when(jnp.logical_not(has_before))
    def _():
        for near in (dk_near, dv_near):
            near[pl.ds(0, SP)] = jnp.zeros((SP, TILE, HD), BF)

    @pl.when(jnp.logical_not(has_after))
    def _():
        for near in (dk_near, dv_near):
            near[pl.ds(SP, SP)] = jnp.zeros((SP, TILE, HD), BF)

    def own_step(n):
        m = me.nth_tile(SP - 1 - n)
        grad_k, grad_v = key_tile(SP + m, query_of, pair_of, q_scaled, g_scaled, probs, dscores)
        for a, (_, near) in enumerate(grads):

            @pl.when(has_before)
            def _():
                landed(near.at[m], grad_got.at[a, m])

            @pl.when(has_after)
            def _():
                landed(near.at[SP + m], grad_got.at[a, SP + m])

        dk_low[m] = (grad_k + dk_near[m].astype(F32) + dk_near[SP + m].astype(F32)).astype(BF)
        dv_low[m] = (grad_v + dv_near[m].astype(F32) + dv_near[SP + m].astype(F32)).astype(BF)
        for part in (2 * m, 2 * m + 1):
            push_back(6, dk_low, dk_out, part)
            push_back(7, dv_low, dv_out, part)

    loop(SP, own_step)

    def drain_far(n):
        for a, (far, _) in enumerate(grads):

            @pl.when(jnp.where(n < SP, has_before, has_after))
            def _():
                landed(far.at[n], grad_sent.at[a, n])

    loop(2 * SP, drain_far)

    for a, (_, dst, first) in enumerate(arrivals):

        def drain(n):
            @pl.when(jnp.logical_not(me.is_me(me.worker_of_mine(n))))
            def _():
                landed(half_rows(dst, me.mine, first), sent.at[a, n])

        loop(HEADS, drain)

    for a, (src, dst) in enumerate(((o, o_out), (dq, dq_out), (dk_low, dk_out), (dv_low, dv_out))):

        def finish(i):
            landed(head_columns(dst, i), got.at[4 + a, i])

            @pl.when(jnp.logical_not(me.is_me(me.holder(i))))
            def _():
                landed(half_rows(src, i), sent.at[4 + a, i])

        loop(HEADS, finish)


def write_kernel(*refs):
    sources, targets, held, sems = refs[:4], refs[4:8], refs[8:12], refs[12]
    reads = [pltpu.make_async_copy(src, mid, sems.at[0, n]) for n, (src, mid) in enumerate(zip(sources, held))]
    writes = [pltpu.make_async_copy(mid, dst, sems.at[1, n]) for n, (mid, dst) in enumerate(zip(held, targets))]
    for read in reads:
        read.start()
    for read, write in zip(reads, writes):
        read.wait()
        write.start()
    for write in writes:
        write.wait()


def body(queries, key_rows, value_rows, grad_out, windows, tile_place):
    anywhere = pl.BlockSpec(memory_space=pl.ANY)
    smem = pl.BlockSpec(memory_space=pltpu.SMEM)
    tiles = lambda n: pltpu.VMEM((n, TILE, HD), BF)
    pairs = pltpu.VMEM((NONE + 1, TILE, TILE), BF)
    numbers = lambda n: pltpu.SMEM((n,), jnp.int32)
    dma = pltpu.SemaphoreType.DMA
    rows = jax.ShapeDtypeStruct(queries.shape, BF)
    results = pl.pallas_call(
        attention_kernel,
        out_shape=[rows] * 4,
        in_specs=[smem] * 2 + [anywhere] * 4,
        out_specs=[anywhere] * 4,
        scratch_shapes=[tiles(SP), tiles(3 * SP), tiles(3 * SP), tiles(SP), tiles(SP), tiles(SP)]
        + [pltpu.VMEM((SP, HD, TILE), BF), pltpu.VMEM((SP, 1, TILE), F32), pairs, pairs]
        + [tiles(SP)] * 2
        + [tiles(2 * SP)] * 4
        + [tiles(SP)] * 2
        + [numbers(3 * SP), numbers(SP * W), numbers(SP * W), numbers(9 * SP), numbers(9 * SP)]
        + [dma((8, HEADS)), dma((8, HEADS)), dma((2, 2 * SP)), dma((2, 2 * SP)), dma((2, 2 * SP)), dma((2, 2 * SP))],
        compiler_params=pltpu.CompilerParams(
            collective_id=0, has_side_effects=True, vmem_limit_bytes=56 * 1024 * 1024
        ),
        name="attention",
    )(windows.T, tile_place.T, queries, key_rows, value_rows, grad_out)
    return pl.pallas_call(
        write_kernel,
        out_shape=[rows] * 4,
        in_specs=[anywhere] * 4,
        out_specs=[anywhere] * 4,
        scratch_shapes=[pltpu.VMEM(queries.shape, BF)] * 4 + [dma((2, 4))],
        name="write",
    )(*results)


def solution(mesh):
    spread = P(("tm", "head"), None)
    return jax.shard_map(
        body,
        mesh=mesh,
        in_specs=(spread,) * 4 + (P(), P()),
        out_specs=(spread,) * 4,
        check_vma=False,
    )
```

```python
import functools

import jax
import jax.numpy as jnp
import numpy as np
from jax import lax
from jax.sharding import PartitionSpec as P
import jax.experimental.pallas as pl
import jax.experimental.pallas.tpu as pltpu

HD = 128
HEADS = 16
TILE = 256
SP = 8
W = 6
HALF = 128
NONE = SP * W
MESH = pl.DeviceIdType.MESH
BF = jnp.bfloat16
F32 = jnp.float32
SCALE = HD**-0.5
SCALE2 = float(SCALE * np.log2(np.e))
NN = (((1,), (0,)), ((), ()))
TN = (((0,), (0,)), ((), ()))


def dot(a, b, dims):
    return lax.dot_general(a, b, dims, preferred_element_type=F32)


class Place:
    def __init__(self):
        self.tm = lax.axis_index("tm")
        self.index = lax.axis_index("head")
        self.low, self.y = self.tm // 4, lax.rem(self.tm, 4)
        self.x = x = self.index // 8
        self.z = z = 2 * lax.rem(self.index // 2, 4) + self.low
        self.half, self.mine = self.index // HEADS, lax.rem(self.index, HEADS)
        self.core = lax.rem(self.index, 2)
        self.head = 8 * (x // 2) + z
        self.group = 4 * lax.rem(x + z, 2) + self.y
        self.slice = 2 * self.group + self.core
        self.last = 2 * lax.axis_size("tm") - 1
        self.stays = (self.group == self.tm) & (self.core == self.half)

    def worker(self, group, head, core):
        z = lax.rem(head, 8)
        x = 2 * (head // 8) + lax.rem(group // 4 + z, 2)
        return 4 * lax.rem(z, 2) + lax.rem(group, 4), 8 * x + 2 * (z // 2) + core

    def worker_of_mine(self, head):
        return self.worker(self.tm, head, self.half)

    def holder(self, i):
        return self.group, HEADS * self.core + i

    def is_me(self, device):
        return (device[0] == self.tm) & (device[1] == self.index)

    def nth_head(self, n):
        step = n // 2
        far = (step + 1) // 2
        turn = jnp.where(lax.rem(step + self.core, 2) == 1, far, 8 - far)
        return 8 * lax.rem(self.head // 8 + n, 2) + lax.rem(self.head + turn, 8)

    def nth_tile(self, n):
        step = n // 2
        even = lax.rem(self.z + self.group // 4, 2) == 0
        near = jnp.where(even, jnp.where(step == 1, 2, 0), jnp.where(step == 1, 7, 1))
        far = jnp.where(even, jnp.where(step == 2, 6, 4), jnp.where(step == 2, 3, 5))
        z = lax.rem(self.z + jnp.where(step < 2, near, far), 8)
        return 4 * lax.rem(self.x + n, 2) + z // 2

    def before(self):
        return self.worker(self.group - 1 + self.core, self.head, 1 - self.core)

    def after(self):
        return self.worker(self.group + self.core, self.head, 1 - self.core)


def greet(me):
    barrier = pltpu.get_barrier_semaphore()

    def signal(i):
        for other in (me.worker_of_mine(i), me.holder(i)):

            @pl.when(jnp.logical_not(me.is_me(other)))
            def _():
                pl.semaphore_signal(barrier, 1, device_id=other, device_id_type=MESH)

    for i in range(HEADS):
        signal(jnp.int32(i))
    has_before, has_after = me.slice > 0, me.slice < me.last

    @pl.when(has_before)
    def _():
        pl.semaphore_signal(barrier, 1, device_id=me.before(), device_id_type=MESH)

    @pl.when(has_after)
    def _():
        pl.semaphore_signal(barrier, 1, device_id=me.after(), device_id_type=MESH)

    own = jnp.where(me.stays, 2, 0)
    pl.semaphore_wait(barrier, 2 * HEADS - own + has_before.astype(jnp.int32) + has_after.astype(jnp.int32))


def landed(ref, sem):
    pltpu.make_async_copy(ref, ref, sem).wait()


def send(src, dst, send_sem, recv_sem, target):
    pltpu.make_async_remote_copy(
        src_ref=src, dst_ref=dst, send_sem=send_sem, recv_sem=recv_sem, device_id=target, device_id_type=MESH
    ).start()


def half_rows(ref, i, first=0):
    return ref.at[first + i // 2, pl.ds(pl.multiple_of(lax.rem(i, 2) * HALF, HALF), HALF)]


def head_columns(ref, h):
    return ref.at[:, pl.ds(pl.multiple_of(h * HD, HD), HD)]


def loop(n, step):
    def body(i, carry):
        step(i)
        return carry

    lax.fori_loop(0, n, body, 0)


def tables(me, windows, tile_place, inverse, key_at, usable, query_of, pair_of):
    slice_id, last = me.slice, me.last

    def invert(n):
        near = jnp.clip(slice_id - 1 + n // SP, 0, last)
        tile = lax.rem(n, SP)
        found = jnp.int32(0)
        for i in range(SP):
            found = jnp.where(tile_place[i, near] == tile, i, found)
        inverse[n] = found

    loop(3 * SP, invert)

    def query(n):
        i = n // W
        w = lax.rem(n, W)
        tile = SP * slice_id + jnp.clip(tile_place[i, slice_id], 0, SP - 1)
        listed = windows[w, tile]
        good = listed >= 0
        named = jnp.where(good, listed, windows[2, tile])
        near = jnp.clip(named - SP * (slice_id - 1), 0, 3 * SP - 1)
        key_at[n] = inverse[near] + SP * jnp.where(good, w // 2, 1)
        usable[n] = good.astype(jnp.int32)

    loop(SP * W, query)

    def key(n):
        m = n // 3
        j = m // SP
        near = jnp.clip(slice_id - 1 + j, 0, last)
        tile = jnp.clip(tile_place[lax.rem(m, SP), near], 0, SP - 1)
        row = tile // 2 + lax.rem(n, 3) - 1
        inside = (row >= 0) & (row < SP // 2)
        asker = jnp.where(inside, 2 * row + lax.rem(tile, 2), 0)
        i = inverse[SP + asker]
        name = SP * near + tile
        first = windows[2 * j, SP * slice_id + asker] == name
        second = windows[2 * j + 1, SP * slice_id + asker] == name
        query_of[n] = i
        pair_of[n] = jnp.where(
            inside & (first | second), i * W + 2 * j + jnp.where(second, 1, 0), NONE
        )

    loop(9 * SP, key)


def forward_tile(i, key_at, usable, q, kx, vx, o, o_turned, share, probs, q_scaled):
    q_rows = q[i]
    q_turned = q_rows.T
    at = [key_at[i * W + w] for w in range(W)]
    scores = [dot(kx[at[w]], q_turned, NN) for w in range(W)]
    peak = scores[0]
    for w in range(1, W):
        peak = jnp.maximum(peak, scores[w])
    peak = jnp.max(peak, axis=0, keepdims=True) * SCALE2
    total = jnp.zeros((1, TILE), F32)
    out = jnp.zeros((HD, TILE), F32)
    for w in range(W):
        level = peak + jnp.where(usable[i * W + w] > 0, 0.0, 1e30)
        e = jnp.exp2(scores[w] * SCALE2 - level)
        total = total + jnp.sum(e, axis=0, keepdims=True)
        low = e.astype(BF)
        probs[i * W + w] = low
        out = out + dot(vx[at[w]], low, TN)
    part = 1.0 / total
    out_low = (out * part).astype(BF)
    share[i] = part
    o_turned[i] = out_low
    o[i] = out_low.T
    part_rows = jnp.transpose(jnp.broadcast_to(part, (HD, TILE)))
    q_scaled[i] = (q_rows.astype(F32) * (part_rows * SCALE)).astype(BF)


def backward_tile(i, key_at, g, kx, vx, dq, o_turned, share, probs, dscores, g_scaled):
    g_rows = g[i]
    g_turned = g_rows.T
    at = [key_at[i * W + w] for w in range(W)]
    part = share[i]
    row_term = jnp.sum(g_turned.astype(F32) * o_turned[i].astype(F32), axis=0, keepdims=True)
    grad = jnp.zeros((HD, TILE), F32)
    for w in range(W):
        dprobs = dot(vx[at[w]], g_turned, NN)
        low = (probs[i * W + w].astype(F32) * (dprobs - row_term)).astype(BF)
        dscores[i * W + w] = low
        grad = grad + dot(kx[at[w]], low, TN)
    dq[i] = (grad * (part * SCALE)).astype(BF).T
    part_rows = jnp.transpose(jnp.broadcast_to(part, (HD, TILE)))
    g_scaled[i] = (g_rows.astype(F32) * part_rows).astype(BF)


def key_tile(m, query_of, pair_of, q_scaled, g_scaled, probs, dscores):
    grad_k = jnp.zeros((TILE, HD), F32)
    grad_v = jnp.zeros((TILE, HD), F32)
    for n in range(3):
        i = query_of[3 * m + n]
        pair = pair_of[3 * m + n]
        grad_v = grad_v + dot(probs[pair], g_scaled[i], NN)
        grad_k = grad_k + dot(dscores[pair], q_scaled[i], NN)
    return grad_k, grad_v


def attention_kernel(
    windows, tile_place, q_in, k_in, v_in, g_in, o_out, dq_out, dk_out, dv_out,
    q, kx, vx, g, o, dq, o_turned, share, probs, dscores, q_scaled, g_scaled, dk_far, dv_far, dk_near, dv_near,
    dk_low, dv_low, inverse, key_at, usable, query_of, pair_of, sent, got, halo_sent, halo_got, grad_sent, grad_got,
):
    me = Place()
    has_before, has_after = me.slice > 0, me.slice < me.last
    greet(me)

    arrivals = ((k_in, kx, SP), (v_in, vx, SP), (q_in, q, 0), (g_in, g, 0))
    def push_all(a):
        src, dst, first = arrivals[a]

        def push(n):
            h = me.nth_head(HEADS - 1 - n)
            target = me.worker_of_mine(h)
            to = half_rows(dst, me.mine, first)

            @pl.when(jnp.logical_not(me.is_me(target)))
            def _():
                send(head_columns(src, h), to, sent.at[a, h], got.at[a, me.mine], target)

            @pl.when(me.is_me(target))
            def _():
                pltpu.make_async_copy(head_columns(src, h), to, got.at[a, me.mine]).start()

        loop(HEADS, push)

    for a in (0, 1, 2, 3):
        push_all(a)
    tables(me, windows, tile_place, inverse, key_at, usable, query_of, pair_of)
    probs[NONE] = jnp.zeros((TILE, TILE), BF)
    dscores[NONE] = jnp.zeros((TILE, TILE), BF)

    def pass_on(a, n):
        src, x, first = arrivals[a]
        i = me.nth_tile(SP - 1 - n)
        for part in (2 * i, 2 * i + 1):
            landed(half_rows(x, part, SP), got.at[a, part])

        @pl.when(has_before)
        def _():
            send(x.at[SP + i], x.at[2 * SP + i], halo_sent.at[a, i], halo_got.at[a, SP + i], me.before())

        @pl.when(has_after)
        def _():
            send(x.at[SP + i], x.at[i], halo_sent.at[a, SP + i], halo_got.at[a, i], me.after())

    def passed_on(a, i):
        x = arrivals[a][1]

        @pl.when(has_before)
        def _():
            landed(x.at[i], halo_got.at[a, i])
            landed(x.at[SP + i], halo_sent.at[a, i])

        @pl.when(has_after)
        def _():
            landed(x.at[2 * SP + i], halo_got.at[a, SP + i])
            landed(x.at[SP + i], halo_sent.at[a, SP + i])

    for a in (0, 1):
        loop(SP, functools.partial(pass_on, a))
    for a in (0, 1):
        loop(SP, functools.partial(passed_on, a))

    def push_back(a, src, dst, i):
        target = me.holder(i)
        to = head_columns(dst, me.head)

        @pl.when(jnp.logical_not(me.is_me(target)))
        def _():
            send(half_rows(src, i), to, sent.at[a, i], got.at[a, me.head], target)

        @pl.when(me.is_me(target))
        def _():
            pltpu.make_async_copy(half_rows(src, i), to, got.at[a, me.head]).start()

    def forward_step(n):
        i = me.nth_tile(SP - 1 - n)
        for part in (2 * i, 2 * i + 1):
            landed(half_rows(q, part), got.at[2, part])
        forward_tile(i, key_at, usable, q, kx, vx, o, o_turned, share, probs, q_scaled)
        for part in (2 * i, 2 * i + 1):
            push_back(4, o, o_out, part)

    def backward_step(n):
        i = me.nth_tile(SP - 1 - n)
        for part in (2 * i, 2 * i + 1):
            landed(half_rows(g, part), got.at[3, part])
        backward_tile(i, key_at, g, kx, vx, dq, o_turned, share, probs, dscores, g_scaled)
        for part in (2 * i, 2 * i + 1):
            push_back(5, dq, dq_out, part)

    loop(SP, forward_step)
    loop(SP, backward_step)

    def far_step(k):
        n = lax.rem(k + SP * me.core, 2 * SP)
        m = jnp.where(n < SP, n, n + SP)
        grad_k, grad_v = key_tile(m, query_of, pair_of, q_scaled, g_scaled, probs, dscores)
        dk_far[n] = grad_k.astype(BF)
        dv_far[n] = grad_v.astype(BF)
        there = lax.rem(n + SP, 2 * SP)
        for a, (far, near) in enumerate(grads):

            @pl.when((n < SP) & has_before)
            def _():
                send(far.at[n], near.at[there], grad_sent.at[a, n], grad_got.at[a, there], me.before())

            @pl.when((n >= SP) & has_after)
            def _():
                send(far.at[n], near.at[there], grad_sent.at[a, n], grad_got.at[a, there], me.after())

    grads = ((dk_far, dk_near), (dv_far, dv_near))
    loop(2 * SP, far_step)

    @pl.when(jnp.logical_not(has_before))
    def _():
        for near in (dk_near, dv_near):
            near[pl.ds(0, SP)] = jnp.zeros((SP, TILE, HD), BF)

    @pl.when(jnp.logical_not(has_after))
    def _():
        for near in (dk_near, dv_near):
            near[pl.ds(SP, SP)] = jnp.zeros((SP, TILE, HD), BF)

    def own_step(n):
        m = me.nth_tile(SP - 1 - n)
        grad_k, grad_v = key_tile(SP + m, query_of, pair_of, q_scaled, g_scaled, probs, dscores)
        for a, (_, near) in enumerate(grads):

            @pl.when(has_before)
            def _():
                landed(near.at[m], grad_got.at[a, m])

            @pl.when(has_after)
            def _():
                landed(near.at[SP + m], grad_got.at[a, SP + m])

        dk_low[m] = (grad_k + dk_near[m].astype(F32) + dk_near[SP + m].astype(F32)).astype(BF)
        dv_low[m] = (grad_v + dv_near[m].astype(F32) + dv_near[SP + m].astype(F32)).astype(BF)
        for part in (2 * m, 2 * m + 1):
            push_back(6, dk_low, dk_out, part)
            push_back(7, dv_low, dv_out, part)

    loop(SP, own_step)

    def drain_far(n):
        for a, (far, _) in enumerate(grads):

            @pl.when(jnp.where(n < SP, has_before, has_after))
            def _():
                landed(far.at[n], grad_sent.at[a, n])

    loop(2 * SP, drain_far)

    for a, (_, dst, first) in enumerate(arrivals):

        def drain(n):
            @pl.when(jnp.logical_not(me.is_me(me.worker_of_mine(n))))
            def _():
                landed(half_rows(dst, me.mine, first), sent.at[a, n])

        loop(HEADS, drain)

    for a, (src, dst) in enumerate(((o, o_out), (dq, dq_out), (dk_low, dk_out), (dv_low, dv_out))):

        def finish(i):
            landed(head_columns(dst, i), got.at[4 + a, i])

            @pl.when(jnp.logical_not(me.is_me(me.holder(i))))
            def _():
                landed(half_rows(src, i), sent.at[4 + a, i])

        loop(HEADS, finish)


def write_kernel(*refs):
    sources, targets, held, sems = refs[:4], refs[4:8], refs[8:12], refs[12]
    reads = [pltpu.make_async_copy(src, mid, sems.at[0, n]) for n, (src, mid) in enumerate(zip(sources, held))]
    writes = [pltpu.make_async_copy(mid, dst, sems.at[1, n]) for n, (mid, dst) in enumerate(zip(held, targets))]
    for read in reads:
        read.start()
    for read, write in zip(reads, writes):
        read.wait()
        write.start()
    for write in writes:
        write.wait()


def body(queries, key_rows, value_rows, grad_out, windows, tile_place):
    anywhere = pl.BlockSpec(memory_space=pl.ANY)
    smem = pl.BlockSpec(memory_space=pltpu.SMEM)
    tiles = lambda n: pltpu.VMEM((n, TILE, HD), BF)
    pairs = pltpu.VMEM((NONE + 1, TILE, TILE), BF)
    numbers = lambda n: pltpu.SMEM((n,), jnp.int32)
    dma = pltpu.SemaphoreType.DMA
    rows = jax.ShapeDtypeStruct(queries.shape, BF)
    results = pl.pallas_call(
        attention_kernel,
        out_shape=[rows] * 4,
        in_specs=[smem] * 2 + [anywhere] * 4,
        out_specs=[anywhere] * 4,
        scratch_shapes=[tiles(SP), tiles(3 * SP), tiles(3 * SP), tiles(SP), tiles(SP), tiles(SP)]
        + [pltpu.VMEM((SP, HD, TILE), BF), pltpu.VMEM((SP, 1, TILE), F32), pairs, pairs]
        + [tiles(SP)] * 2
        + [tiles(2 * SP)] * 4
        + [tiles(SP)] * 2
        + [numbers(3 * SP), numbers(SP * W), numbers(SP * W), numbers(9 * SP), numbers(9 * SP)]
        + [dma((8, HEADS)), dma((8, HEADS)), dma((2, 2 * SP)), dma((2, 2 * SP)), dma((2, 2 * SP)), dma((2, 2 * SP))],
        compiler_params=pltpu.CompilerParams(
            collective_id=0, has_side_effects=True, vmem_limit_bytes=56 * 1024 * 1024
        ),
        name="attention",
    )(windows.T, tile_place.T, queries, key_rows, value_rows, grad_out)
    return pl.pallas_call(
        write_kernel,
        out_shape=[rows] * 4,
        in_specs=[anywhere] * 4,
        out_specs=[anywhere] * 4,
        scratch_shapes=[pltpu.VMEM(queries.shape, BF)] * 4 + [dma((2, 4))],
        name="write",
    )(*results)


def solution(mesh):
    spread = P(("tm", "head"), None)
    return jax.shard_map(
        body,
        mesh=mesh,
        in_specs=(spread,) * 4 + (P(), P()),
        out_specs=(spread,) * 4,
        check_vma=False,
    )
```
